32 devices in a mesh: src: 16 (over z, y, core), att: 2 (over x).
Axes of the slice: x: 2, y: 2, z: 4, core: 2. Of those that a mesh axis runs over, the one named last changes fastest.
Arguments:
- attitude: float32 [4, 512], P(None, 'att'), may hold values from -6 to 6
- obs_value: float32 [1048576], P(('src', 'att')), may hold values from -192 to 192
- obs_weight: float32 [1048576], P(('src', 'att')), may hold values from 0.5 to 5
- obs_time: float32 [1048576], P(('src', 'att')), may hold values from 0 to 1
- att_partials: float32 [4, 1048576], P(None, ('src', 'att')), may hold values from -6 to 6
- src_partials: float32 [5, 1048576], P(None, ('src', 'att')), may hold values from -6 to 6
- obs_source: int32 [1048576], P(('src', 'att')), may hold values from 0 to 4095
- knot_start: int32 [8192], P(('src', 'att')), may hold values from 0 to 508, as said below
- valid_count: int32 [8192], P(('src', 'att')), may hold values from 32 to 128
Outputs:
- attitude_step: float32 [4, 512], P(None, 'att')
- source_step: float32 [5, 65536], P(None, 'src')
The draws below stay inside these ranges and needn't reach their ends.
Inputs may be any that keep to these rules, and one draw needn't show every extreme that they name: `obs_source`: index among the 4096 sources of the observation's src shard. `knot_start`: the blocks of a device at index a of att start in knots a * 256 to a * 256 + 256 - 1 (the segment that att index owns). `valid_count`: rows past the count are padding.
All inputs are finite; a program needn't handle non-finite values.
Results may differ from the reference program's by a relative error of at most 0.0003.
Values sent between devices are 32-bit elements; how exact they have to be, the bound alone decides.
A program may use at most 64 MiB of HBM per device.

```python
import math
import jax
import jax.numpy as jnp
from jax import lax

BLK = 128
NBLK_DEV = 256
KCH = 256
ITERS = 4
SRC_DEV = 4096
KNOTS = 512
OBS = 1048576
NBLKS = 8192
N_SRC = 16
N_ATT = 2


def draw_knot_start(key, part):
    key = jax.random.fold_in(key, 11)
    block = jnp.arange(NBLKS, dtype=jnp.int32)
    segment = block // NBLK_DEV % N_ATT
    offset = jax.random.randint(key, (NBLKS,), 0, KCH, dtype=jnp.int32)
    return jnp.minimum(segment * KCH + offset, KNOTS - 4).astype(jnp.int32)


def place_ends(drawn, own_key, low, largest):
    shape = drawn.shape
    index_at = [jax.random.randint(jax.random.fold_in(own_key, axis), (), 0, shape[axis]) for axis in range(len(shape))]
    drawn = drawn.at[tuple(index_at)].set(low)
    longest = shape.index(max(shape))
    index_at[longest] = (index_at[longest] + 1) % shape[longest]
    return drawn.at[tuple(index_at)].set(largest)


def level_of(rng, shape, shards, least, largest):
    gain = 1.0
    for axis_at, parts in shards:
        heights = jax.random.uniform(jax.random.fold_in(jax.random.fold_in(rng, 6), axis_at), (parts,), jnp.float32, least / len(shards), largest / len(shards))
        gain = gain * jnp.repeat(jnp.exp(heights), shape[axis_at] // parts).reshape((-1,) + (1,) * (len(shape) - 1 - axis_at))
    return gain


def noise(own_key, dims, spread, most, split=(), held_as=jnp.bfloat16):
    array = spread * jax.random.normal(own_key, dims, jnp.float32)
    if split:
        array = array * level_of(own_key, dims, split, -0.22, 0.18)
    return jnp.clip(array, -most, most).astype(held_as)


def setup_inputs(seed: int = 0) -> dict:
    streams_of = jax.random.split(jax.random.key(seed), 10)
    attitude = noise(streams_of[0], (4, KNOTS), 1.0, 6.0, ((1, 2),), jnp.float32)
    obs_value = noise(streams_of[1], (OBS,), 32.0, 192.0, ((0, 32),), jnp.float32)
    obs_weight = jnp.clip(jnp.exp(math.log(5.0) - 2.3025851 * jax.random.uniform(streams_of[2], (OBS,), jnp.float32) ** level_of(streams_of[2], (OBS,), ((0, 32),), -0.2, 0.2)), 0.5, 5.0)
    obs_time = jnp.clip(1.0 * jax.random.uniform(streams_of[3], (OBS,), jnp.float32) ** level_of(streams_of[3], (OBS,), ((0, 32),), -0.2, 0.2), 0.0, 1.0)
    att_partials = noise(streams_of[4], (4, OBS), 1.0, 6.0, ((1, 32),), jnp.float32)
    src_partials = noise(streams_of[5], (5, OBS), 1.0, 6.0, ((1, 32),), jnp.float32)
    obs_source = place_ends(jax.random.randint(streams_of[6], (OBS,), 0, SRC_DEV), jax.random.fold_in(streams_of[6], 1), 0, SRC_DEV - 1).astype(jnp.int32)
    knot_start = draw_knot_start(jax.random.fold_in(streams_of[9], 71), 0)
    valid_count = place_ends(jax.random.randint(streams_of[8], (NBLKS,), 32, BLK + 1), jax.random.fold_in(streams_of[8], 1), 32, BLK).astype(jnp.int32)
    return dict(attitude=attitude, obs_value=obs_value, obs_weight=obs_weight, obs_time=obs_time, att_partials=att_partials, src_partials=src_partials, obs_source=obs_source, knot_start=knot_start, valid_count=valid_count)


OMEGA = 0.2
ATT_PRIOR = 1.0
SRC_PRIOR = 1.0
HIGH = lax.Precision.HIGHEST


def spline_basis(phase):
    rest = 1.0 - phase
    square = phase * phase
    cube = square * phase
    return jnp.stack([rest * rest * rest / 6.0, (3.0 * cube - 6.0 * square + 4.0) / 6.0,
                      (-3.0 * cube + 3.0 * square + 3.0 * phase + 1.0) / 6.0, cube / 6.0])


def pick_knots(attitude_full, knot_start):
    index = knot_start[:, None] + jnp.arange(4, dtype=jnp.int32)[None, :]
    return attitude_full[:, index]


def predict(att_blocks, basis, picked):
    return jnp.einsum('ibr,jbr,ibj->br', att_blocks, basis, picked, precision=HIGH)


def block_terms(att_blocks, basis, weight, resid):
    nblock = weight.shape[0]
    design = (att_blocks[:, None] * basis[None, :]).reshape(16, nblock, weight.shape[1])
    weighted = design * weight[None]
    gram = jnp.einsum('kbr,lbr->bkl', weighted, design, precision=HIGH)
    hvec = jnp.einsum('kbr,br->bk', weighted, resid, precision=HIGH)
    return gram, hvec


def block_rows(gram, hvec, knot_start):
    nblock = gram.shape[0]
    grams = gram.reshape(nblock, 4, 4, 4, 4)
    hparts = hvec.reshape(nblock, 4, 4)
    zeros = jnp.zeros((nblock, 4, 4), jnp.float32)
    row_sets = []
    for leading in range(4):
        pieces = []
        for distance in range(4):
            if leading + distance <= 3:
                pieces.append(grams[:, :, leading, :, leading + distance])
            else:
                pieces.append(zeros)
        banded = jnp.stack(pieces, axis=1).reshape(nblock, 64)
        row_sets.append(jnp.concatenate([banded, hparts[:, :, leading]], axis=1))
    stacked = jnp.stack(row_sets, axis=0).reshape(4 * nblock, 68)
    knot_ids = (knot_start[None, :] + jnp.arange(4, dtype=jnp.int32)[:, None]).reshape(4 * nblock)
    return stacked, knot_ids


def apply_band(band, band_ext, padded, count):
    image = jnp.zeros((4, count), jnp.float32)
    for distance in range(4):
        upper = padded[:, 3 + distance:3 + distance + count]
        image = image + jnp.einsum('ijk,jk->ik', band[distance], upper, precision=HIGH)
        if distance > 0:
            lower_band = band_ext[distance][:, :, 3 - distance:3 - distance + count]
            lower_step = padded[:, 3 - distance:3 - distance + count]
            image = image + jnp.einsum('jik,jk->ik', lower_band, lower_step, precision=HIGH)
    return image


def solve_small(matrix, vector):
    entries = [[matrix[line, column] for column in range(5)] for line in range(5)]
    target = [vector[line] for line in range(5)]
    for pivot in range(5):
        for line in range(pivot + 1, 5):
            factor = entries[line][pivot] / entries[pivot][pivot]
            for column in range(pivot, 5):
                entries[line][column] = entries[line][column] - factor * entries[pivot][column]
            target[line] = target[line] - factor * target[pivot]
    result = [None] * 5
    for line in reversed(range(5)):
        total = target[line]
        for column in range(line + 1, 5):
            total = total - entries[line][column] * result[column]
        result[line] = total / entries[line][line]
    return jnp.stack(result)


def source_terms(partials, weight, resid):
    count = weight.shape[0]
    weighted = partials * weight[None, :]
    outer = (weighted[:, None, :] * partials[None, :, :]).reshape(25, count)
    right = weighted * resid[None, :]
    return jnp.concatenate([outer, right], axis=0).T


def finish_sources(sums):
    count = sums.shape[0]
    matrix = sums[:, :25].T.reshape(5, 5, count) + SRC_PRIOR * jnp.eye(5, dtype=jnp.float32)[:, :, None]
    return solve_small(matrix, sums[:, 25:].T)


def device_blocks(attitude_full, values, weights, times, att_dev, knot_dev, valid_dev):
    nblock = knot_dev.shape[0]
    width = values.shape[0] // nblock
    basis = spline_basis(times.reshape(nblock, width))
    position = jnp.arange(width, dtype=jnp.int32)[None, :]
    weight = jnp.where(position < valid_dev[:, None], weights.reshape(nblock, width), 0.0)
    att_blocks = att_dev.reshape(4, nblock, width)
    grid = values.reshape(nblock, width)
    return basis, weight, att_blocks, grid


def reference(attitude, obs_value, obs_weight, obs_time, att_partials, src_partials, obs_source, knot_start, valid_count):
    devices = N_SRC * N_ATT
    values_all = obs_value.reshape(devices, -1)
    weights_all = obs_weight.reshape(devices, -1)
    times_all = obs_time.reshape(devices, -1)
    att_all = jnp.transpose(att_partials.reshape(4, devices, -1), (1, 0, 2))
    src_all = jnp.transpose(src_partials.reshape(5, devices, -1), (1, 0, 2))
    ids_all = obs_source.reshape(devices, -1)
    knots_all = knot_start.reshape(devices, -1)
    valid_all = valid_count.reshape(devices, -1)

    def first_pass(items):
        values, weights, times, att_dev, knot_dev, valid_dev = items
        basis, weight, att_blocks, grid = device_blocks(attitude, values, weights, times, att_dev, knot_dev, valid_dev)
        resid = grid - predict(att_blocks, basis, pick_knots(attitude, knot_dev))
        gram, hvec = block_terms(att_blocks, basis, weight, resid)
        return block_rows(gram, hvec, knot_dev)

    rows, knot_ids = lax.map(first_pass, (values_all, weights_all, times_all, att_all, knots_all, valid_all))
    knot_total = attitude.shape[1]
    summed = jax.ops.segment_sum(rows.reshape(-1, 68), knot_ids.reshape(-1), num_segments=knot_total).T
    band = summed[:64].reshape(4, 4, 4, knot_total)
    rhs = summed[64:]
    band_ext = jnp.pad(band, ((0, 0), (0, 0), (0, 0), (3, 0)))
    diagonal = band[0, jnp.arange(4), jnp.arange(4), :] + ATT_PRIOR
    step = jnp.zeros((4, knot_total), jnp.float32)
    for sweep in range(ITERS):
        padded = jnp.pad(step, ((0, 0), (3, 3)))
        image = apply_band(band, band_ext, padded, knot_total) + ATT_PRIOR * step
        step = step + OMEGA * (rhs - image) / diagonal
    updated = attitude + step

    def second_pass(items):
        values, weights, times, att_dev, knot_dev, valid_dev, src_dev, ids_dev = items
        basis, weight, att_blocks, grid = device_blocks(updated, values, weights, times, att_dev, knot_dev, valid_dev)
        resid = grid - predict(att_blocks, basis, pick_knots(updated, knot_dev))
        terms = source_terms(src_dev, weight.reshape(-1), resid.reshape(-1))
        return jax.ops.segment_sum(terms, ids_dev, num_segments=SRC_DEV)

    sums = lax.map(second_pass, (values_all, weights_all, times_all, att_all, knots_all, valid_all, src_all, ids_all))
    sums = sums.reshape(N_SRC, N_ATT, SRC_DEV, 30).sum(axis=1).reshape(N_SRC * SRC_DEV, 30)
    return step, finish_sources(sums)
```

```python
import functools

import jax
import jax.numpy as jnp
from jax import lax
from jax.experimental import pallas as pl
from jax.experimental.pallas import tpu as pltpu
from jax.sharding import PartitionSpec as P

ITERS = 4
SRC_DEV = 4096
OMEGA = 0.2
ATT_PRIOR = 1.0
SRC_PRIOR = 1.0
HIGH = lax.Precision.HIGHEST
MESH = pl.DeviceIdType.MESH

PAIRS = [(i, j) for i in range(4) for j in range(i, 4)]
PAIR_AT = {}
for _n, (_i, _j) in enumerate(PAIRS):
    PAIR_AT[(_i, _j)] = _n
    PAIR_AT[(_j, _i)] = _n
BAND_ROWS = 48
USED_ROWS = 44
STEP = 512
HI = 256
LO = SRC_DEV // HI


def basis_of(u):
    rest = 1.0 - u
    square = u * u
    cube = square * u
    return [
        rest * rest * rest / 6.0,
        (3.0 * cube - 6.0 * square + 4.0) / 6.0,
        (-3.0 * cube + 3.0 * square + 3.0 * u + 1.0) / 6.0,
        cube / 6.0,
    ]


def dot_last(a, b, precision=None):
    return lax.dot_general(
        a, b, (((1,), (1,)), ((), ())), precision=precision, preferred_element_type=jnp.float32
    )


def kernel(
    n_src,
    n_att,
    att_ref,
    val_ref,
    wgt_ref,
    time_ref,
    apart_ref,
    spart_ref,
    ids_ref,
    knot_ref,
    valid_ref,
    step_ref,
    out_ref,
    vt,
    pt,
    bt,
    wr,
    rr,
    wpp,
    zrows,
    part,
    slots,
    full,
    left,
    right,
    att_left,
    att_right,
    acc_s,
    acc_g,
    s_slots,
    g_slots,
    rs_send,
    rs_recv,
    ag_send,
    ag_recv,
    l_send,
    l_recv,
    r_send,
    r_recv,
    a_send,
    a_recv,
    s_send,
    s_recv,
    g_send,
    g_recv,
):
    me = lax.axis_index("src")
    seg = lax.axis_index("att")
    per = part.shape[1]
    nblock, width = val_ref.shape
    count = att_ref.shape[1]
    barrier = pltpu.get_barrier_semaphore()

    def greet(t, carry):
        pl.semaphore_signal(
            barrier,
            inc=1,
            device_id=(lax.rem(me + t, n_src), seg),
            device_id_type=MESH,
        )
        return carry

    lax.fori_loop(1, n_src, greet, 0)
    for t in range(1, n_att):

        def greet_across(s, carry, t=t):
            pl.semaphore_signal(
                barrier, inc=1, device_id=(s, lax.rem(seg + t, n_att)), device_id_type=MESH
            )
            return carry

        lax.fori_loop(0, n_src, greet_across, 0)

    position = lax.broadcasted_iota(jnp.int32, (width, nblock), 0)
    weight = jnp.where(position < valid_ref[...], wgt_ref[...].T, 0.0)
    wr[...] = weight.T
    vt[0] = weight
    value = val_ref[...].T
    vt[1] = value
    basis = basis_of(time_ref[...].T)
    for j in range(4):
        bt[j] = basis[j]
        pt[j] = apart_ref[j].T
    wvalue = weight * value
    for n, (i, j) in enumerate(PAIRS):
        wpp[n] = weight * pt[i] * pt[j]
    for i in range(4):
        wpp[10 + i] = wvalue * pt[i]
    zrows[...] = jnp.zeros_like(zrows)
    for j0 in range(4):
        for d in range(4 - j0):
            both = bt[j0] * bt[j0 + d]
            for n in range(10):
                row = j0 * BAND_ROWS + d * 10 + n
                zrows[row : row + 1, :] = jnp.sum(wpp[n] * both, axis=0, keepdims=True)
        for i in range(4):
            row = j0 * BAND_ROWS + 40 + i
            zrows[row : row + 1, :] = jnp.sum(wpp[10 + i] * bt[j0], axis=0, keepdims=True)
    local = knot_ref[...] - seg * count
    knots = lax.broadcasted_iota(jnp.int32, (count, nblock), 0)
    hot = jnp.where(knots == local, 1.0, 0.0)
    placed = dot_last(zrows[...], hot, HIGH)
    placed = jnp.concatenate(
        [placed, jnp.zeros((4 * BAND_ROWS, 128), jnp.float32)], axis=1
    )
    rows = placed[:BAND_ROWS]
    for j0 in range(1, 4):
        rows = rows + pltpu.roll(placed[j0 * BAND_ROWS : (j0 + 1) * BAND_ROWS], j0, 1)
    for c in range(n_src):
        top = min((c + 1) * per, BAND_ROWS)
        if c * per < BAND_ROWS:
            if top - c * per == per:
                part[c] = rows[c * per : top]
            else:
                part[c] = jnp.zeros(part.shape[1:], jnp.float32)
                part[c, : top - c * per] = rows[c * per : top]
        else:
            part[c] = jnp.zeros(part.shape[1:], jnp.float32)

    pl.semaphore_wait(barrier, n_src * n_att - 1)

    def rs_copy(t):
        c = lax.rem(me + t, n_src)
        return pltpu.make_async_remote_copy(
            src_ref=part.at[c],
            dst_ref=slots.at[me],
            send_sem=rs_send.at[c],
            recv_sem=rs_recv.at[me],
            device_id=(c, seg),
            device_id_type=MESH,
        )

    def rs_wait(t):
        s = lax.rem(me + t, n_src)
        return pltpu.make_async_remote_copy(
            src_ref=part.at[s],
            dst_ref=slots.at[s],
            send_sem=rs_send.at[s],
            recv_sem=rs_recv.at[s],
            device_id=(s, seg),
            device_id_type=MESH,
        )

    def att_copy(dst, slot, shift):
        return pltpu.make_async_remote_copy(
            src_ref=att_ref,
            dst_ref=dst,
            send_sem=a_send.at[slot],
            recv_sem=a_recv.at[slot],
            device_id=(me, lax.rem(seg + shift + n_att, n_att)),
            device_id_type=MESH,
        )

    def run(make):
        def body(t, carry):
            make(t).start()
            return carry

        return body

    def finish(make):
        def body(t, carry):
            make(t).wait()
            return carry

        return body

    slots[me] = part[me]
    lax.fori_loop(1, n_src, run(rs_copy), 0)
    to_right = att_copy(att_left, 0, 1)
    to_left = att_copy(att_right, 1, -1)
    to_right.start()
    to_left.start()

    lanes = lax.broadcasted_iota(jnp.int32, (HI, 1), 0).astype(jnp.float32)
    blocks = STEP // width

    def row_of(ref, g):
        return jnp.concatenate(
            [ref[pl.ds(g * blocks + t, 1), :] for t in range(blocks)], axis=1
        )

    def hot_pair(g):
        ids = row_of(ids_ref, g)
        low = jnp.bitwise_and(ids, HI - 1).astype(jnp.float32).astype(jnp.bfloat16)
        high = jnp.right_shift(ids, 8).astype(jnp.float32).astype(jnp.bfloat16)
        base = jnp.broadcast_to(low, (HI, STEP))
        lane_hot = jnp.where(
            base == jnp.broadcast_to(lanes.astype(jnp.bfloat16), (HI, STEP)),
            jnp.bfloat16(1),
            jnp.bfloat16(0),
        )
        return lane_hot, jnp.broadcast_to(high, (16, STEP))

    def spread(terms, high):
        parts = []
        zero = jnp.zeros((16, STEP), jnp.bfloat16)
        for line in range(LO):
            mask = high == jnp.bfloat16(line)
            for term in terms:
                parts.append(jnp.where(mask, term, zero))
        return jnp.concatenate(parts, axis=0)

    def s_step(g, carry):
        lane_hot, high = hot_pair(g)
        p = spart_ref[:, pl.ds(pl.multiple_of(g * STEP, STEP), STEP)]
        wp = p * row_of(wr, g)
        p1 = jnp.concatenate([p[1:], p[:1]], axis=0)
        p2 = jnp.concatenate([p[2:], p[:2]], axis=0)
        terms = jnp.concatenate(
            [wp * p, wp * p1, wp * p2, jnp.zeros((1, STEP), jnp.float32)], axis=0
        )
        coarse = terms.astype(jnp.bfloat16)
        fine = (terms - coarse.astype(jnp.float32)).astype(jnp.bfloat16)
        got = dot_last(spread([coarse, fine], high), lane_hot)
        acc_s[0] += got[:, :128]
        acc_s[1] += got[:, 128:]
        return carry

    steps = nblock * width // STEP
    acc_s[...] = jnp.zeros_like(acc_s)
    lax.fori_loop(0, steps // 2, s_step, 0)

    lax.fori_loop(1, n_src, finish(rs_wait), 0)
    total = slots[0]
    for s in range(1, n_src):
        total = total + slots[s]
    full[me] = total

    def ag_copy(t):
        c = lax.rem(me + t, n_src)
        return pltpu.make_async_remote_copy(
            src_ref=full.at[me],
            dst_ref=full.at[me],
            send_sem=ag_send.at[c],
            recv_sem=ag_recv.at[me],
            device_id=(c, seg),
            device_id_type=MESH,
        )

    def ag_wait(t):
        s = lax.rem(me + t, n_src)
        return pltpu.make_async_remote_copy(
            src_ref=full.at[s],
            dst_ref=full.at[s],
            send_sem=ag_send.at[s],
            recv_sem=ag_recv.at[s],
            device_id=(s, seg),
            device_id_type=MESH,
        )

    def right_copy(c, slot):
        return pltpu.make_async_remote_copy(
            src_ref=full.at[slot, :, pl.ds(count - 128, 256)],
            dst_ref=left.at[slot],
            send_sem=r_send.at[c],
            recv_sem=r_recv.at[slot],
            device_id=(c, lax.rem(seg + 1, n_att)),
            device_id_type=MESH,
        )

    def left_copy(c, slot):
        return pltpu.make_async_remote_copy(
            src_ref=full.at[slot, :, pl.ds(0, 128)],
            dst_ref=right.at[slot],
            send_sem=l_send.at[c],
            recv_sem=l_recv.at[slot],
            device_id=(c, lax.rem(seg + n_att - 1, n_att)),
            device_id_type=MESH,
        )

    lax.fori_loop(1, n_src, run(ag_copy), 0)

    @pl.when(seg < n_att - 1)
    def _():
        lax.fori_loop(0, n_src, run(lambda t: right_copy(lax.rem(me + t, n_src), me)), 0)

    @pl.when(seg > 0)
    def _():
        lax.fori_loop(0, n_src, run(lambda t: left_copy(lax.rem(me + t, n_src), me)), 0)

    lax.fori_loop(steps // 2, steps, s_step, 0)

    def mine(buf, c, half):
        return buf[c, :, half * 128 : half * 128 + 128]

    for c in range(15):
        for half in range(2):
            s_slots[seg, c, :, half * 128 : half * 128 + 128] = (
                acc_s[half, pl.ds(c, LO, stride=32), :]
                + acc_s[half, pl.ds(16 + c, LO, stride=32), :]
            )

    def across(buf, send, recv, t, slot):
        return pltpu.make_async_remote_copy(
            src_ref=buf.at[slot],
            dst_ref=buf.at[slot],
            send_sem=send.at[t],
            recv_sem=recv.at[slot],
            device_id=(me, lax.rem(seg + t, n_att)),
            device_id_type=MESH,
        )

    for t in range(1, n_att):
        across(s_slots, s_send, s_recv, t, seg).start()

    lax.fori_loop(1, n_src, finish(ag_wait), 0)

    @pl.when(seg < n_att - 1)
    def _():
        def body(t, carry):
            right_copy(t, me).wait_send()
            left_copy(t, t).wait_recv()
            return carry

        lax.fori_loop(0, n_src, body, 0)

    @pl.when(seg > 0)
    def _():
        def body(t, carry):
            left_copy(t, me).wait_send()
            right_copy(t, t).wait_recv()
            return carry

        lax.fori_loop(0, n_src, body, 0)

    @pl.when(seg == 0)
    def _():
        left[...] = jnp.zeros_like(left)

    @pl.when(seg == n_att - 1)
    def _():
        right[...] = jnp.zeros_like(right)

    to_right.wait()
    to_left.wait()

    def wide(row):
        c, t = divmod(row, per)
        own = full[c, t : t + 1, :]
        before = left[c, t : t + 1, :]
        after = right[c, t : t + 1, :]
        return jnp.concatenate(
            [
                before[:, :128],
                own[:, :128] + before[:, 128:],
                own[:, 128:count],
                own[:, count:] + after,
            ],
            axis=1,
        )

    line = [wide(row) for row in range(USED_ROWS)]
    band = [
        [
            jnp.concatenate([line[d * 10 + PAIR_AT[(i, j)]] for i in range(4)], axis=0)
            for j in range(4)
        ]
        for d in range(4)
    ]
    right_side = jnp.concatenate(line[40:44], axis=0)
    diagonal = (
        jnp.concatenate([line[PAIR_AT[(i, i)]] for i in range(4)], axis=0) + ATT_PRIOR
    )
    span = count + 256
    zero_halo = jnp.zeros((4, 128), jnp.float32)
    coeff = jnp.concatenate(
        [
            jnp.where(seg > 0, att_left[:, count - 128 :], zero_halo),
            att_ref[...],
            jnp.where(seg < n_att - 1, att_right[:, :128], zero_halo),
        ],
        axis=1,
    )

    def apply(vec):
        image = jnp.zeros_like(vec)
        for d in range(4):
            ahead = vec if d == 0 else pltpu.roll(vec, span - d, 1)
            low = jnp.zeros_like(vec)
            for j in range(4):
                image = image + band[d][j] * ahead[j : j + 1]
                if d > 0:
                    low = low + band[d][j] * vec[j : j + 1]
            if d > 0:
                image = image + pltpu.roll(low, d, 1)
        return image

    right_side = right_side - apply(coeff)
    step = OMEGA * right_side / diagonal
    for _ in range(ITERS - 1):
        step = step + OMEGA * (right_side - apply(step) - ATT_PRIOR * step) / diagonal
    step_ref[...] = step[:, 128 : 128 + count]
    updated = coeff + step
    shifted = jnp.concatenate(
        [
            (updated if j == 0 else pltpu.roll(updated, span - j, 1))[:, 128 : 128 + count]
            for j in range(4)
        ],
        axis=0,
    )
    hot2 = jnp.where(
        lax.broadcasted_iota(jnp.int32, (count, nblock), 0) == knot_ref[...] - seg * count, 1.0, 0.0
    )
    picked = lax.dot_general(
        shifted,
        hot2,
        (((1,), (0,)), ((), ())),
        precision=HIGH,
        preferred_element_type=jnp.float32,
    )
    resid = vt[1]
    for i in range(4):
        knot_sum = jnp.zeros((width, nblock), jnp.float32)
        for j in range(4):
            knot_sum = knot_sum + bt[j] * picked[j * 4 + i : j * 4 + i + 1]
        resid = resid - pt[i] * knot_sum
    rr[...] = (vt[0] * resid).T

    def g_step(g, carry):
        lane_hot, high = hot_pair(g)
        p = spart_ref[:, pl.ds(pl.multiple_of(g * STEP, STEP), STEP)]
        terms = jnp.concatenate(
            [p * row_of(rr, g), jnp.zeros((3, STEP), jnp.float32)], axis=0
        )
        coarse = terms.astype(jnp.bfloat16).astype(jnp.float32)
        both = jnp.concatenate([coarse, terms - coarse], axis=0).astype(jnp.bfloat16)
        got = dot_last(spread([both], high), lane_hot)
        acc_g[0] += got[:, :128]
        acc_g[1] += got[:, 128:]
        return carry

    acc_g[...] = jnp.zeros_like(acc_g)
    lax.fori_loop(0, steps, g_step, 0)
    for c in range(5):
        for half in range(2):
            g_slots[seg, c, :, half * 128 : half * 128 + 128] = (
                acc_g[half, pl.ds(c, LO, stride=16), :]
                + acc_g[half, pl.ds(8 + c, LO, stride=16), :]
            )
    for t in range(1, n_att):
        across(g_slots, g_send, g_recv, t, seg).start()

    def collect(buf, send, recv):
        for t in range(1, n_att):
            across(buf, send, recv, t, seg).wait_send()
            across(buf, send, recv, t, lax.rem(seg + t, n_att)).wait_recv()

    collect(s_slots, s_send, s_recv)

    def summed(buf, c):
        got = buf[0, c]
        for a in range(1, n_att):
            got = got + buf[a, c]
        return got

    entries = [[None] * 5 for _ in range(5)]
    for k in range(3):
        for i in range(5):
            got = summed(s_slots, k * 5 + i)
            other = (i + k) % 5
            if k == 0:
                got = got + SRC_PRIOR
            entries[i][other] = got
            entries[other][i] = got
    factors = {}
    for pivot in range(5):
        for row in range(pivot + 1, 5):
            factor = entries[row][pivot] / entries[pivot][pivot]
            factors[(row, pivot)] = factor
            for column in range(pivot + 1, 5):
                entries[row][column] = entries[row][column] - factor * entries[pivot][column]

    collect(g_slots, g_send, g_recv)
    target = [summed(g_slots, c) for c in range(5)]
    for pivot in range(5):
        for row in range(pivot + 1, 5):
            target[row] = target[row] - factors[(row, pivot)] * target[pivot]
    result = [None] * 5
    for row in reversed(range(5)):
        got = target[row]
        for column in range(row + 1, 5):
            got = got - entries[row][column] * result[column]
        result[row] = got / entries[row][row]
    for c in range(5):
        for a in range(LO):
            out_ref[c : c + 1, a * HI : (a + 1) * HI] = result[c][a : a + 1, :]


def solution(mesh):
    n_src = mesh.shape["src"]
    n_att = mesh.shape["att"]

    def shards(
        attitude,
        obs_value,
        obs_weight,
        obs_time,
        att_partials,
        src_partials,
        obs_source,
        knot_start,
        valid_count,
    ):
        nblock = knot_start.shape[0]
        width = obs_value.shape[0] // nblock
        count = attitude.shape[1]
        per = -(-USED_ROWS // n_src)
        f32 = jnp.float32
        dma = pltpu.SemaphoreType.DMA
        vmem = pl.BlockSpec(memory_space=pltpu.VMEM)
        tall = (width, nblock)
        return pl.pallas_call(
            functools.partial(kernel, n_src, n_att),
            out_shape=(
                jax.ShapeDtypeStruct((4, count), f32),
                jax.ShapeDtypeStruct((5, SRC_DEV), f32),
            ),
            in_specs=[vmem] * 9,
            out_specs=(vmem, vmem),
            scratch_shapes=[
                pltpu.VMEM((2,) + tall, f32),
                pltpu.VMEM((4,) + tall, f32),
                pltpu.VMEM((4,) + tall, f32),
                pltpu.VMEM((nblock, width), f32),
                pltpu.VMEM((nblock, width), f32),
                pltpu.VMEM((14,) + tall, f32),
                pltpu.VMEM((4 * BAND_ROWS, nblock), f32),
                pltpu.VMEM((n_src, per, count + 128), f32),
                pltpu.VMEM((n_src, per, count + 128), f32),
                pltpu.VMEM((n_src, per, count + 128), f32),
                pltpu.VMEM((n_src, per, 256), f32),
                pltpu.VMEM((n_src, per, 128), f32),
                pltpu.VMEM((4, count), f32),
                pltpu.VMEM((4, count), f32),
                pltpu.VMEM((2, LO * 32, 128), f32),
                pltpu.VMEM((2, LO * 16, 128), f32),
                pltpu.VMEM((n_att, 15, LO, HI), f32),
                pltpu.VMEM((n_att, 5, LO, HI), f32),
                dma((n_src,)),
                dma((n_src,)),
                dma((n_src,)),
                dma((n_src,)),
                dma((n_src,)),
                dma((n_src,)),
                dma((n_src,)),
                dma((n_src,)),
                dma((2,)),
                dma((2,)),
                dma((n_att,)),
                dma((n_att,)),
                dma((n_att,)),
                dma((n_att,)),
            ],
            compiler_params=pltpu.CompilerParams(
                collective_id=0,
                has_side_effects=True,
                vmem_limit_bytes=48 * 1024 * 1024,
            ),
        )(
            attitude,
            obs_value.reshape(nblock, width),
            obs_weight.reshape(nblock, width),
            obs_time.reshape(nblock, width),
            att_partials.reshape(4, nblock, width),
            src_partials,
            obs_source.reshape(nblock, width),
            knot_start.reshape(1, nblock),
            valid_count.reshape(1, nblock),
        )

    in_specs = (
        P(None, "att"),
        P(("src", "att")),
        P(("src", "att")),
        P(("src", "att")),
        P(None, ("src", "att")),
        P(None, ("src", "att")),
        P(("src", "att")),
        P(("src", "att")),
        P(("src", "att")),
    )
    out_specs = (P(None, "att"), P(None, "src"))
    return jax.shard_map(shards, mesh=mesh, in_specs=in_specs, out_specs=out_specs, check_vma=False)
```

```python
import functools

import jax
import jax.numpy as jnp
from jax import lax
from jax.experimental import pallas as pl
from jax.experimental.pallas import tpu as pltpu
from jax.sharding import PartitionSpec as P

ITERS = 4
SRC_DEV = 4096
OMEGA = 0.2
ATT_PRIOR = 1.0
SRC_PRIOR = 1.0
HIGH = lax.Precision.HIGHEST
MESH = pl.DeviceIdType.MESH

PAIRS = [(i, j) for i in range(4) for j in range(i, 4)]
PAIR_AT = {}
for _n, (_i, _j) in enumerate(PAIRS):
    PAIR_AT[(_i, _j)] = _n
    PAIR_AT[(_j, _i)] = _n
BAND_ROWS = 48
USED_ROWS = 44
STEP = 4096
HI = 256
LO = SRC_DEV // HI


def basis_of(u):
    rest = 1.0 - u
    square = u * u
    cube = square * u
    return [
        rest * rest * rest / 6.0,
        (3.0 * cube - 6.0 * square + 4.0) / 6.0,
        (-3.0 * cube + 3.0 * square + 3.0 * u + 1.0) / 6.0,
        cube / 6.0,
    ]


def dot_last(a, b, precision=None):
    return lax.dot_general(
        a, b, (((1,), (1,)), ((), ())), precision=precision, preferred_element_type=jnp.float32
    )


def kernel(
    n_src,
    n_att,
    att_ref,
    val_hbm,
    wgt_hbm,
    time_hbm,
    apart_hbm,
    spart_hbm,
    ids_hbm,
    knot_ref,
    valid_ref,
    step_ref,
    out_ref,
    val_ref,
    wgt_ref,
    time_ref,
    apart_ref,
    spart_ref,
    ids_ref,
    in_sem,
    mixed,
    vt,
    pt,
    bt,
    wr,
    rr,
    wpp,
    zrows,
    part,
    slots,
    full,
    left,
    right,
    att_left,
    att_right,
    acc_s,
    acc_g,
    s_slots,
    g_slots,
    rs_send,
    rs_recv,
    ag_send,
    ag_recv,
    l_send,
    l_recv,
    r_send,
    r_recv,
    a_send,
    a_recv,
    s_send,
    s_recv,
    g_send,
    g_recv,
):
    me = lax.axis_index("src")
    seg = lax.axis_index("att")
    per = part.shape[1]
    nblock, width = val_hbm.shape
    count = att_ref.shape[1]
    barrier = pltpu.get_barrier_semaphore()
    loads = [
        pltpu.make_async_copy(source, place, in_sem.at[n])
        for n, (source, place) in enumerate(
            [
                (apart_hbm, apart_ref),
                (wgt_hbm, wgt_ref),
                (time_hbm, time_ref),
                (val_hbm, val_ref),
                (spart_hbm, spart_ref),
                (ids_hbm, ids_ref),
            ]
        )
    ]
    for load in loads:
        load.start()

    def greet(t, carry):
        pl.semaphore_signal(
            barrier,
            inc=1,
            device_id=(lax.rem(me + t, n_src), seg),
            device_id_type=MESH,
        )
        return carry

    lax.fori_loop(1, n_src, greet, 0)
    for t in range(1, n_att):

        def greet_across(s, carry, t=t):
            pl.semaphore_signal(
                barrier, inc=1, device_id=(s, lax.rem(seg + t, n_att)), device_id_type=MESH
            )
            return carry

        lax.fori_loop(0, n_src, greet_across, 0)

    loads[0].wait()

    def mix(g, carry):
        for t in range(8):
            at = pl.multiple_of((g * 8 + t) * 2 * width, 2 * width)
            both = apart_ref[:, pl.ds(at, 2 * width)]
            mixed[pl.ds(pl.multiple_of((g * 8 + t) * 8, 8), 8), :] = jnp.concatenate(
                [both[:, :width], both[:, width:]], axis=0
            )
        return carry

    lax.fori_loop(0, nblock // 16, mix, 0)
    for load in loads[1:4]:
        load.wait()
    position = lax.broadcasted_iota(jnp.int32, (width, nblock), 0)
    weight = jnp.where(position < valid_ref[...], wgt_ref[...].T, 0.0)
    wr[...] = weight.T
    vt[0] = weight
    value = val_ref[...].T
    vt[1] = value
    basis = basis_of(time_ref[...].T)
    for j in range(4):
        bt[j] = basis[j]
        pt[j] = mixed[pl.ds(j, nblock, stride=4), :].T
    wvalue = weight * value
    for n, (i, j) in enumerate(PAIRS):
        wpp[n] = weight * pt[i] * pt[j]
    for i in range(4):
        wpp[10 + i] = wvalue * pt[i]
    zrows[...] = jnp.zeros_like(zrows)
    for j0 in range(4):
        for d in range(4 - j0):
            both = bt[j0] * bt[j0 + d]
            for n in range(10):
                row = j0 * BAND_ROWS + d * 10 + n
                zrows[row : row + 1, :] = jnp.sum(wpp[n] * both, axis=0, keepdims=True)
        for i in range(4):
            row = j0 * BAND_ROWS + 40 + i
            zrows[row : row + 1, :] = jnp.sum(wpp[10 + i] * bt[j0], axis=0, keepdims=True)
    local = knot_ref[...] - seg * count
    knots = lax.broadcasted_iota(jnp.int32, (count, nblock), 0)
    hot = jnp.where(knots == local, 1.0, 0.0)
    placed = dot_last(zrows[...], hot, HIGH)
    placed = jnp.concatenate(
        [placed, jnp.zeros((4 * BAND_ROWS, 128), jnp.float32)], axis=1
    )
    rows = placed[:BAND_ROWS]
    for j0 in range(1, 4):
        rows = rows + pltpu.roll(placed[j0 * BAND_ROWS : (j0 + 1) * BAND_ROWS], j0, 1)
    for c in range(n_src):
        top = min((c + 1) * per, BAND_ROWS)
        if c * per < BAND_ROWS:
            if top - c * per == per:
                part[c] = rows[c * per : top]
            else:
                part[c] = jnp.zeros(part.shape[1:], jnp.float32)
                part[c, : top - c * per] = rows[c * per : top]
        else:
            part[c] = jnp.zeros(part.shape[1:], jnp.float32)

    pl.semaphore_wait(barrier, n_src * n_att - 1)

    def rs_copy(t):
        c = lax.rem(me + t, n_src)
        return pltpu.make_async_remote_copy(
            src_ref=part.at[c],
            dst_ref=slots.at[me],
            send_sem=rs_send.at[c],
            recv_sem=rs_recv.at[me],
            device_id=(c, seg),
            device_id_type=MESH,
        )

    def rs_wait(t):
        s = lax.rem(me + t, n_src)
        return pltpu.make_async_remote_copy(
            src_ref=part.at[s],
            dst_ref=slots.at[s],
            send_sem=rs_send.at[s],
            recv_sem=rs_recv.at[s],
            device_id=(s, seg),
            device_id_type=MESH,
        )

    def att_copy(dst, slot, shift):
        return pltpu.make_async_remote_copy(
            src_ref=att_ref,
            dst_ref=dst,
            send_sem=a_send.at[slot],
            recv_sem=a_recv.at[slot],
            device_id=(me, lax.rem(seg + shift + n_att, n_att)),
            device_id_type=MESH,
        )

    def run(make):
        def body(t, carry):
            make(t).start()
            return carry

        return body

    def finish(make):
        def body(t, carry):
            make(t).wait()
            return carry

        return body

    slots[me] = part[me]
    lax.fori_loop(1, n_src, run(rs_copy), 0)
    to_right = att_copy(att_left, 0, 1)
    to_left = att_copy(att_right, 1, -1)
    to_right.start()
    to_left.start()

    lanes = lax.broadcasted_iota(jnp.int32, (HI, 1), 0).astype(jnp.float32)
    blocks = STEP // width

    def row_of(ref, g):
        return jnp.concatenate(
            [ref[pl.ds(g * blocks + t, 1), :] for t in range(blocks)], axis=1
        )

    def hot_pair(g):
        ids = row_of(ids_ref, g)
        low = jnp.bitwise_and(ids, HI - 1).astype(jnp.float32).astype(jnp.bfloat16)
        high = jnp.right_shift(ids, 8).astype(jnp.float32).astype(jnp.bfloat16)
        base = jnp.broadcast_to(low, (HI, STEP))
        lane_hot = jnp.where(
            base == jnp.broadcast_to(lanes.astype(jnp.bfloat16), (HI, STEP)),
            jnp.bfloat16(1),
            jnp.bfloat16(0),
        )
        return lane_hot, jnp.broadcast_to(high, (16, STEP))

    def spread(terms, high):
        parts = []
        zero = jnp.zeros((16, STEP), jnp.bfloat16)
        for line in range(LO):
            mask = high == jnp.bfloat16(line)
            for term in terms:
                parts.append(jnp.where(mask, term, zero))
        return jnp.concatenate(parts, axis=0)

    def s_step(g, carry):
        lane_hot, high = hot_pair(g)
        p = spart_ref[:, pl.ds(pl.multiple_of(g * STEP, STEP), STEP)]
        wp = p * row_of(wr, g)
        p1 = jnp.concatenate([p[1:], p[:1]], axis=0)
        p2 = jnp.concatenate([p[2:], p[:2]], axis=0)
        terms = jnp.concatenate(
            [wp * p, wp * p1, wp * p2, jnp.zeros((1, STEP), jnp.float32)], axis=0
        )
        coarse = terms.astype(jnp.bfloat16)
        fine = (terms - coarse.astype(jnp.float32)).astype(jnp.bfloat16)
        got = dot_last(spread([coarse, fine], high), lane_hot)
        acc_s[0] += got[:, :128]
        acc_s[1] += got[:, 128:]
        return carry

    steps = nblock * width // STEP
    acc_s[...] = jnp.zeros_like(acc_s)
    loads[4].wait()
    loads[5].wait()
    lax.fori_loop(0, steps // 2, s_step, 0)

    lax.fori_loop(1, n_src, finish(rs_wait), 0)
    total = slots[0]
    for s in range(1, n_src):
        total = total + slots[s]
    full[me] = total

    def ag_copy(t):
        c = lax.rem(me + t, n_src)
        return pltpu.make_async_remote_copy(
            src_ref=full.at[me],
            dst_ref=full.at[me],
            send_sem=ag_send.at[c],
            recv_sem=ag_recv.at[me],
            device_id=(c, seg),
            device_id_type=MESH,
        )

    def ag_wait(t):
        s = lax.rem(me + t, n_src)
        return pltpu.make_async_remote_copy(
            src_ref=full.at[s],
            dst_ref=full.at[s],
            send_sem=ag_send.at[s],
            recv_sem=ag_recv.at[s],
            device_id=(s, seg),
            device_id_type=MESH,
        )

    def right_copy(c, slot):
        return pltpu.make_async_remote_copy(
            src_ref=full.at[slot, :, pl.ds(count - 128, 256)],
            dst_ref=left.at[slot],
            send_sem=r_send.at[c],
            recv_sem=r_recv.at[slot],
            device_id=(c, lax.rem(seg + 1, n_att)),
            device_id_type=MESH,
        )

    def left_copy(c, slot):
        return pltpu.make_async_remote_copy(
            src_ref=full.at[slot, :, pl.ds(0, 128)],
            dst_ref=right.at[slot],
            send_sem=l_send.at[c],
            recv_sem=l_recv.at[slot],
            device_id=(c, lax.rem(seg + n_att - 1, n_att)),
            device_id_type=MESH,
        )

    lax.fori_loop(1, n_src, run(ag_copy), 0)

    @pl.when(seg < n_att - 1)
    def _():
        lax.fori_loop(0, n_src, run(lambda t: right_copy(lax.rem(me + t, n_src), me)), 0)

    @pl.when(seg > 0)
    def _():
        lax.fori_loop(0, n_src, run(lambda t: left_copy(lax.rem(me + t, n_src), me)), 0)

    lax.fori_loop(steps // 2, steps, s_step, 0)

    def mine(buf, c, half):
        return buf[c, :, half * 128 : half * 128 + 128]

    for c in range(15):
        for half in range(2):
            s_slots[seg, c, :, half * 128 : half * 128 + 128] = (
                acc_s[half, pl.ds(c, LO, stride=32), :]
                + acc_s[half, pl.ds(16 + c, LO, stride=32), :]
            )

    def across(buf, send, recv, t, slot):
        return pltpu.make_async_remote_copy(
            src_ref=buf.at[slot],
            dst_ref=buf.at[slot],
            send_sem=send.at[t],
            recv_sem=recv.at[slot],
            device_id=(me, lax.rem(seg + t, n_att)),
            device_id_type=MESH,
        )

    for t in range(1, n_att):
        across(s_slots, s_send, s_recv, t, seg).start()

    lax.fori_loop(1, n_src, finish(ag_wait), 0)

    @pl.when(seg < n_att - 1)
    def _():
        def body(t, carry):
            right_copy(t, me).wait_send()
            left_copy(t, t).wait_recv()
            return carry

        lax.fori_loop(0, n_src, body, 0)

    @pl.when(seg > 0)
    def _():
        def body(t, carry):
            left_copy(t, me).wait_send()
            right_copy(t, t).wait_recv()
            return carry

        lax.fori_loop(0, n_src, body, 0)

    @pl.when(seg == 0)
    def _():
        left[...] = jnp.zeros_like(left)

    @pl.when(seg == n_att - 1)
    def _():
        right[...] = jnp.zeros_like(right)

    to_right.wait()
    to_left.wait()

    def wide(row):
        c, t = divmod(row, per)
        own = full[c, t : t + 1, :]
        before = left[c, t : t + 1, :]
        after = right[c, t : t + 1, :]
        return jnp.concatenate(
            [
                before[:, :128],
                own[:, :128] + before[:, 128:],
                own[:, 128:count],
                own[:, count:] + after,
            ],
            axis=1,
        )

    line = [wide(row) for row in range(USED_ROWS)]
    band = [
        [
            jnp.concatenate([line[d * 10 + PAIR_AT[(i, j)]] for i in range(4)], axis=0)
            for j in range(4)
        ]
        for d in range(4)
    ]
    right_side = jnp.concatenate(line[40:44], axis=0)
    diagonal = (
        jnp.concatenate([line[PAIR_AT[(i, i)]] for i in range(4)], axis=0) + ATT_PRIOR
    )
    span = count + 256
    zero_halo = jnp.zeros((4, 128), jnp.float32)
    coeff = jnp.concatenate(
        [
            jnp.where(seg > 0, att_left[:, count - 128 :], zero_halo),
            att_ref[...],
            jnp.where(seg < n_att - 1, att_right[:, :128], zero_halo),
        ],
        axis=1,
    )

    def apply(vec):
        image = jnp.zeros_like(vec)
        for d in range(4):
            ahead = vec if d == 0 else pltpu.roll(vec, span - d, 1)
            low = jnp.zeros_like(vec)
            for j in range(4):
                image = image + band[d][j] * ahead[j : j + 1]
                if d > 0:
                    low = low + band[d][j] * vec[j : j + 1]
            if d > 0:
                image = image + pltpu.roll(low, d, 1)
        return image

    right_side = right_side - apply(coeff)
    step = OMEGA * right_side / diagonal
    for _ in range(ITERS - 1):
        step = step + OMEGA * (right_side - apply(step) - ATT_PRIOR * step) / diagonal
    step_ref[...] = step[:, 128 : 128 + count]
    updated = coeff + step
    shifted = jnp.concatenate(
        [
            (updated if j == 0 else pltpu.roll(updated, span - j, 1))[:, 128 : 128 + count]
            for j in range(4)
        ],
        axis=0,
    )
    hot2 = jnp.where(
        lax.broadcasted_iota(jnp.int32, (count, nblock), 0) == knot_ref[...] - seg * count, 1.0, 0.0
    )
    picked = lax.dot_general(
        shifted,
        hot2,
        (((1,), (0,)), ((), ())),
        precision=HIGH,
        preferred_element_type=jnp.float32,
    )
    resid = vt[1]
    for i in range(4):
        knot_sum = jnp.zeros((width, nblock), jnp.float32)
        for j in range(4):
            knot_sum = knot_sum + bt[j] * picked[j * 4 + i : j * 4 + i + 1]
        resid = resid - pt[i] * knot_sum
    rr[...] = (vt[0] * resid).T

    def g_step(g, carry):
        lane_hot, high = hot_pair(g)
        p = spart_ref[:, pl.ds(pl.multiple_of(g * STEP, STEP), STEP)]
        terms = jnp.concatenate(
            [p * row_of(rr, g), jnp.zeros((3, STEP), jnp.float32)], axis=0
        )
        coarse = terms.astype(jnp.bfloat16).astype(jnp.float32)
        both = jnp.concatenate([coarse, terms - coarse], axis=0).astype(jnp.bfloat16)
        got = dot_last(spread([both], high), lane_hot)
        acc_g[0] += got[:, :128]
        acc_g[1] += got[:, 128:]
        return carry

    acc_g[...] = jnp.zeros_like(acc_g)
    lax.fori_loop(0, steps, g_step, 0)
    for c in range(5):
        for half in range(2):
            g_slots[seg, c, :, half * 128 : half * 128 + 128] = (
                acc_g[half, pl.ds(c, LO, stride=16), :]
                + acc_g[half, pl.ds(8 + c, LO, stride=16), :]
            )
    for t in range(1, n_att):
        across(g_slots, g_send, g_recv, t, seg).start()

    def collect(buf, send, recv):
        for t in range(1, n_att):
            across(buf, send, recv, t, seg).wait_send()
            across(buf, send, recv, t, lax.rem(seg + t, n_att)).wait_recv()

    collect(s_slots, s_send, s_recv)

    def summed(buf, c):
        got = buf[0, c]
        for a in range(1, n_att):
            got = got + buf[a, c]
        return got

    entries = [[None] * 5 for _ in range(5)]
    for k in range(3):
        for i in range(5):
            got = summed(s_slots, k * 5 + i)
            other = (i + k) % 5
            if k == 0:
                got = got + SRC_PRIOR
            entries[i][other] = got
            entries[other][i] = got
    factors = {}
    for pivot in range(5):
        for row in range(pivot + 1, 5):
            factor = entries[row][pivot] / entries[pivot][pivot]
            factors[(row, pivot)] = factor
            for column in range(pivot + 1, 5):
                entries[row][column] = entries[row][column] - factor * entries[pivot][column]

    collect(g_slots, g_send, g_recv)
    target = [summed(g_slots, c) for c in range(5)]
    for pivot in range(5):
        for row in range(pivot + 1, 5):
            target[row] = target[row] - factors[(row, pivot)] * target[pivot]
    result = [None] * 5
    for row in reversed(range(5)):
        got = target[row]
        for column in range(row + 1, 5):
            got = got - entries[row][column] * result[column]
        result[row] = got / entries[row][row]
    for c in range(5):
        for a in range(LO):
            out_ref[c : c + 1, a * HI : (a + 1) * HI] = result[c][a : a + 1, :]


def solution(mesh):
    n_src = mesh.shape["src"]
    n_att = mesh.shape["att"]

    def shards(
        attitude,
        obs_value,
        obs_weight,
        obs_time,
        att_partials,
        src_partials,
        obs_source,
        knot_start,
        valid_count,
    ):
        nblock = knot_start.shape[0]
        width = obs_value.shape[0] // nblock
        count = attitude.shape[1]
        per = -(-USED_ROWS // n_src)
        f32 = jnp.float32
        dma = pltpu.SemaphoreType.DMA
        vmem = pl.BlockSpec(memory_space=pltpu.VMEM)
        hbm = pl.BlockSpec(memory_space=pltpu.HBM)
        tall = (width, nblock)
        return pl.pallas_call(
            functools.partial(kernel, n_src, n_att),
            out_shape=(
                jax.ShapeDtypeStruct((4, count), f32),
                jax.ShapeDtypeStruct((5, SRC_DEV), f32),
            ),
            in_specs=[vmem] + [hbm] * 6 + [vmem] * 2,
            out_specs=(vmem, vmem),
            scratch_shapes=[
                pltpu.VMEM((nblock, width), f32),
                pltpu.VMEM((nblock, width), f32),
                pltpu.VMEM((nblock, width), f32),
                pltpu.VMEM((4, nblock * width), f32),
                pltpu.VMEM((5, nblock * width), f32),
                pltpu.VMEM((nblock, width), jnp.int32),
                dma((6,)),
                pltpu.VMEM((4 * nblock, width), f32),
                pltpu.VMEM((2,) + tall, f32),
                pltpu.VMEM((4,) + tall, f32),
                pltpu.VMEM((4,) + tall, f32),
                pltpu.VMEM((nblock, width), f32),
                pltpu.VMEM((nblock, width), f32),
                pltpu.VMEM((14,) + tall, f32),
                pltpu.VMEM((4 * BAND_ROWS, nblock), f32),
                pltpu.VMEM((n_src, per, count + 128), f32),
                pltpu.VMEM((n_src, per, count + 128), f32),
                pltpu.VMEM((n_src, per, count + 128), f32),
                pltpu.VMEM((n_src, per, 256), f32),
                pltpu.VMEM((n_src, per, 128), f32),
                pltpu.VMEM((4, count), f32),
                pltpu.VMEM((4, count), f32),
                pltpu.VMEM((2, LO * 32, 128), f32),
                pltpu.VMEM((2, LO * 16, 128), f32),
                pltpu.VMEM((n_att, 15, LO, HI), f32),
                pltpu.VMEM((n_att, 5, LO, HI), f32),
                dma((n_src,)),
                dma((n_src,)),
                dma((n_src,)),
                dma((n_src,)),
                dma((n_src,)),
                dma((n_src,)),
                dma((n_src,)),
                dma((n_src,)),
                dma((2,)),
                dma((2,)),
                dma((n_att,)),
                dma((n_att,)),
                dma((n_att,)),
                dma((n_att,)),
            ],
            compiler_params=pltpu.CompilerParams(
                collective_id=0,
                has_side_effects=True,
                vmem_limit_bytes=48 * 1024 * 1024,
            ),
        )(
            attitude,
            obs_value.reshape(nblock, width),
            obs_weight.reshape(nblock, width),
            obs_time.reshape(nblock, width),
            att_partials,
            src_partials,
            obs_source.reshape(nblock, width),
            knot_start.reshape(1, nblock),
            valid_count.reshape(1, nblock),
        )

    in_specs = (
        P(None, "att"),
        P(("src", "att")),
        P(("src", "att")),
        P(("src", "att")),
        P(None, ("src", "att")),
        P(None, ("src", "att")),
        P(("src", "att")),
        P(("src", "att")),
        P(("src", "att")),
    )
    out_specs = (P(None, "att"), P(None, "src"))
    return jax.shard_map(shards, mesh=mesh, in_specs=in_specs, out_specs=out_specs, check_vma=False)
```

```python
import functools

import jax
import jax.numpy as jnp
from jax import lax
from jax.experimental import pallas as pl
from jax.experimental.pallas import tpu as pltpu
from jax.sharding import PartitionSpec as P

ITERS = 4
SRC_DEV = 4096
OMEGA = 0.2
ATT_PRIOR = 1.0
SRC_PRIOR = 1.0
HIGH = lax.Precision.HIGHEST
MESH = pl.DeviceIdType.MESH

PAIRS = [(i, j) for i in range(4) for j in range(i, 4)]
PAIR_AT = {}
for _n, (_i, _j) in enumerate(PAIRS):
    PAIR_AT[(_i, _j)] = _n
    PAIR_AT[(_j, _i)] = _n
BAND_ROWS = 48
USED_ROWS = 44
GIVE_AFTER = 3
STEP = 4096
HI = 256
LO = SRC_DEV // HI


def basis_of(u):
    rest = 1.0 - u
    square = u * u
    cube = square * u
    return [
        rest * rest * rest / 6.0,
        (3.0 * cube - 6.0 * square + 4.0) / 6.0,
        (-3.0 * cube + 3.0 * square + 3.0 * u + 1.0) / 6.0,
        cube / 6.0,
    ]


def dot_last(a, b, precision=None):
    return lax.dot_general(
        a, b, (((1,), (1,)), ((), ())), precision=precision, preferred_element_type=jnp.float32
    )


def kernel(
    n_src,
    n_att,
    att_ref,
    val_hbm,
    wgt_hbm,
    time_hbm,
    apart_hbm,
    spart_hbm,
    ids_hbm,
    knot_ref,
    valid_ref,
    step_ref,
    out_ref,
    val_ref,
    wgt_ref,
    time_ref,
    apart_ref,
    spart_ref,
    ids_ref,
    in_sem,
    mixed,
    vt,
    pt,
    bt,
    wr,
    rr,
    wpp,
    zrows,
    part,
    slots,
    full,
    left,
    right,
    att_left,
    att_right,
    acc_s,
    acc_g,
    s_slots,
    g_slots,
    rs_send,
    rs_recv,
    ag_send,
    ag_recv,
    l_send,
    l_recv,
    r_send,
    r_recv,
    a_send,
    a_recv,
    s_send,
    s_recv,
    g_send,
    g_recv,
):
    me = lax.axis_index("src")
    seg = lax.axis_index("att")
    per = part.shape[1]
    nblock, width = val_hbm.shape
    count = att_ref.shape[1]
    barrier = pltpu.get_barrier_semaphore()
    loads = [
        pltpu.make_async_copy(source, place, in_sem.at[n])
        for n, (source, place) in enumerate(
            [
                (apart_hbm, apart_ref),
                (wgt_hbm, wgt_ref),
                (time_hbm, time_ref),
                (val_hbm, val_ref),
                (spart_hbm, spart_ref),
                (ids_hbm, ids_ref),
            ]
        )
    ]
    for load in loads:
        load.start()

    def greet(t, carry):
        pl.semaphore_signal(
            barrier,
            inc=1,
            device_id=(lax.rem(me + t, n_src), seg),
            device_id_type=MESH,
        )
        return carry

    lax.fori_loop(1, n_src, greet, 0)
    for t in range(1, n_att):

        def greet_across(s, carry, t=t):
            pl.semaphore_signal(
                barrier, inc=1, device_id=(s, lax.rem(seg + t, n_att)), device_id_type=MESH
            )
            return carry

        lax.fori_loop(0, n_src, greet_across, 0)

    loads[0].wait()

    def mix(g, carry):
        for t in range(8):
            at = pl.multiple_of((g * 8 + t) * 2 * width, 2 * width)
            both = apart_ref[:, pl.ds(at, 2 * width)]
            mixed[pl.ds(pl.multiple_of((g * 8 + t) * 8, 8), 8), :] = jnp.concatenate(
                [both[:, :width], both[:, width:]], axis=0
            )
        return carry

    lax.fori_loop(0, nblock // 16, mix, 0)
    for load in loads[1:4]:
        load.wait()
    position = lax.broadcasted_iota(jnp.int32, (width, nblock), 0)
    weight = jnp.where(position < valid_ref[...], wgt_ref[...].T, 0.0)
    wr[...] = weight.T
    vt[0] = weight
    value = val_ref[...].T
    vt[1] = value
    basis = basis_of(time_ref[...].T)
    for j in range(4):
        bt[j] = basis[j]
        pt[j] = mixed[pl.ds(j, nblock, stride=4), :].T
    wvalue = weight * value
    for n, (i, j) in enumerate(PAIRS):
        wpp[n] = weight * pt[i] * pt[j]
    for i in range(4):
        wpp[10 + i] = wvalue * pt[i]
    zrows[...] = jnp.zeros_like(zrows)
    for j0 in range(4):
        for d in range(4 - j0):
            both = bt[j0] * bt[j0 + d]
            for n in range(10):
                row = j0 * BAND_ROWS + d * 10 + n
                zrows[row : row + 1, :] = jnp.sum(wpp[n] * both, axis=0, keepdims=True)
        for i in range(4):
            row = j0 * BAND_ROWS + 40 + i
            zrows[row : row + 1, :] = jnp.sum(wpp[10 + i] * bt[j0], axis=0, keepdims=True)
    local = knot_ref[...] - seg * count
    knots = lax.broadcasted_iota(jnp.int32, (count, nblock), 0)
    hot = jnp.where(knots == local, 1.0, 0.0)
    placed = dot_last(zrows[...], hot, HIGH)
    placed = jnp.concatenate(
        [placed, jnp.zeros((4 * BAND_ROWS, 128), jnp.float32)], axis=1
    )
    rows = placed[:BAND_ROWS]
    for j0 in range(1, 4):
        rows = rows + pltpu.roll(placed[j0 * BAND_ROWS : (j0 + 1) * BAND_ROWS], j0, 1)
    for c in range(n_src):
        top = min((c + 1) * per, BAND_ROWS)
        if c * per < BAND_ROWS:
            if top - c * per == per:
                part[c] = rows[c * per : top]
            else:
                part[c] = jnp.zeros(part.shape[1:], jnp.float32)
                part[c, : top - c * per] = rows[c * per : top]
        else:
            part[c] = jnp.zeros(part.shape[1:], jnp.float32)

    pl.semaphore_wait(barrier, n_src * n_att - 1)

    def rs_copy(t):
        c = lax.rem(me + t, n_src)
        return pltpu.make_async_remote_copy(
            src_ref=part.at[c],
            dst_ref=slots.at[me],
            send_sem=rs_send.at[c],
            recv_sem=rs_recv.at[me],
            device_id=(c, seg),
            device_id_type=MESH,
        )

    def rs_wait(t):
        s = lax.rem(me + t, n_src)
        return pltpu.make_async_remote_copy(
            src_ref=part.at[s],
            dst_ref=slots.at[s],
            send_sem=rs_send.at[s],
            recv_sem=rs_recv.at[s],
            device_id=(s, seg),
            device_id_type=MESH,
        )

    def att_copy(dst, slot, shift):
        return pltpu.make_async_remote_copy(
            src_ref=att_ref,
            dst_ref=dst,
            send_sem=a_send.at[slot],
            recv_sem=a_recv.at[slot],
            device_id=(me, lax.rem(seg + shift + n_att, n_att)),
            device_id_type=MESH,
        )

    def run(make):
        def body(t, carry):
            make(t).start()
            return carry

        return body

    def finish(make):
        def body(t, carry):
            make(t).wait()
            return carry

        return body

    slots[me] = part[me]
    lax.fori_loop(1, n_src, run(rs_copy), 0)
    to_right = att_copy(att_left, 0, 1)
    to_left = att_copy(att_right, 1, -1)
    to_right.start()
    to_left.start()

    lanes = lax.broadcasted_iota(jnp.int32, (HI, 1), 0).astype(jnp.float32)
    blocks = STEP // width

    def row_of(ref, g):
        return jnp.concatenate(
            [ref[pl.ds(g * blocks + t, 1), :] for t in range(blocks)], axis=1
        )

    def hot_pair(g):
        ids = row_of(ids_ref, g)
        low = jnp.bitwise_and(ids, HI - 1).astype(jnp.float32).astype(jnp.bfloat16)
        high = jnp.right_shift(ids, 8).astype(jnp.float32).astype(jnp.bfloat16)
        base = jnp.broadcast_to(low, (HI, STEP))
        lane_hot = jnp.where(
            base == jnp.broadcast_to(lanes.astype(jnp.bfloat16), (HI, STEP)),
            jnp.bfloat16(1),
            jnp.bfloat16(0),
        )
        return lane_hot, jnp.broadcast_to(high, (16, STEP))

    def spread(terms, high):
        parts = []
        zero = jnp.zeros((16, STEP), jnp.bfloat16)
        for line in range(LO):
            mask = high == jnp.bfloat16(line)
            for term in terms:
                parts.append(jnp.where(mask, term, zero))
        return jnp.concatenate(parts, axis=0)

    def s_step(g, carry):
        lane_hot, high = hot_pair(g)
        p = spart_ref[:, pl.ds(pl.multiple_of(g * STEP, STEP), STEP)]
        wp = p * row_of(wr, g)
        p1 = jnp.concatenate([p[1:], p[:1]], axis=0)
        p2 = jnp.concatenate([p[2:], p[:2]], axis=0)
        terms = jnp.concatenate(
            [wp * p, wp * p1, wp * p2, jnp.zeros((1, STEP), jnp.float32)], axis=0
        )
        coarse = terms.astype(jnp.bfloat16)
        fine = (terms - coarse.astype(jnp.float32)).astype(jnp.bfloat16)
        got = dot_last(spread([coarse, fine], high), lane_hot)
        acc_s[0] += got[:, :128]
        acc_s[1] += got[:, 128:]
        return carry

    steps = nblock * width // STEP
    acc_s[...] = jnp.zeros_like(acc_s)
    loads[4].wait()
    loads[5].wait()
    def ag_copy(t):
        c = lax.rem(me + t, n_src)
        return pltpu.make_async_remote_copy(
            src_ref=full.at[me],
            dst_ref=full.at[me],
            send_sem=ag_send.at[c],
            recv_sem=ag_recv.at[me],
            device_id=(c, seg),
            device_id_type=MESH,
        )

    def ag_wait(t):
        s = lax.rem(me + t, n_src)
        return pltpu.make_async_remote_copy(
            src_ref=full.at[s],
            dst_ref=full.at[s],
            send_sem=ag_send.at[s],
            recv_sem=ag_recv.at[s],
            device_id=(s, seg),
            device_id_type=MESH,
        )

    def right_copy(c, slot):
        return pltpu.make_async_remote_copy(
            src_ref=full.at[slot, :, pl.ds(count - 128, 256)],
            dst_ref=left.at[slot],
            send_sem=r_send.at[c],
            recv_sem=r_recv.at[slot],
            device_id=(c, lax.rem(seg + 1, n_att)),
            device_id_type=MESH,
        )

    def left_copy(c, slot):
        return pltpu.make_async_remote_copy(
            src_ref=full.at[slot, :, pl.ds(0, 128)],
            dst_ref=right.at[slot],
            send_sem=l_send.at[c],
            recv_sem=l_recv.at[slot],
            device_id=(c, lax.rem(seg + n_att - 1, n_att)),
            device_id_type=MESH,
        )

    def give():
        lax.fori_loop(1, n_src, finish(rs_wait), 0)
        total = slots[0]
        for s in range(1, n_src):
            total = total + slots[s]
        full[me] = total

        lax.fori_loop(1, n_src, run(ag_copy), 0)

        @pl.when(seg < n_att - 1)
        def _():
            lax.fori_loop(0, n_src, run(lambda t: right_copy(lax.rem(me + t, n_src), me)), 0)

        @pl.when(seg > 0)
        def _():
            lax.fori_loop(0, n_src, run(lambda t: left_copy(lax.rem(me + t, n_src), me)), 0)


    def s_and_give(g, carry):
        s_step(g, carry)
        pl.when(g == GIVE_AFTER)(give)
        return carry

    lax.fori_loop(0, steps, s_and_give, 0)

    def mine(buf, c, half):
        return buf[c, :, half * 128 : half * 128 + 128]

    for c in range(15):
        for half in range(2):
            s_slots[seg, c, :, half * 128 : half * 128 + 128] = (
                acc_s[half, pl.ds(c, LO, stride=32), :]
                + acc_s[half, pl.ds(16 + c, LO, stride=32), :]
            )

    def across(buf, send, recv, t, slot):
        return pltpu.make_async_remote_copy(
            src_ref=buf.at[slot],
            dst_ref=buf.at[slot],
            send_sem=send.at[t],
            recv_sem=recv.at[slot],
            device_id=(me, lax.rem(seg + t, n_att)),
            device_id_type=MESH,
        )

    for t in range(1, n_att):
        across(s_slots, s_send, s_recv, t, seg).start()

    lax.fori_loop(1, n_src, finish(ag_wait), 0)

    @pl.when(seg < n_att - 1)
    def _():
        def body(t, carry):
            right_copy(t, me).wait_send()
            left_copy(t, t).wait_recv()
            return carry

        lax.fori_loop(0, n_src, body, 0)

    @pl.when(seg > 0)
    def _():
        def body(t, carry):
            left_copy(t, me).wait_send()
            right_copy(t, t).wait_recv()
            return carry

        lax.fori_loop(0, n_src, body, 0)

    @pl.when(seg == 0)
    def _():
        left[...] = jnp.zeros_like(left)

    @pl.when(seg == n_att - 1)
    def _():
        right[...] = jnp.zeros_like(right)

    to_right.wait()
    to_left.wait()

    def wide(row):
        c, t = divmod(row, per)
        own = full[c, t : t + 1, :]
        before = left[c, t : t + 1, :]
        after = right[c, t : t + 1, :]
        return jnp.concatenate(
            [
                before[:, :128],
                own[:, :128] + before[:, 128:],
                own[:, 128:count],
                own[:, count:] + after,
            ],
            axis=1,
        )

    line = [wide(row) for row in range(USED_ROWS)]
    band = [
        [
            jnp.concatenate([line[d * 10 + PAIR_AT[(i, j)]] for i in range(4)], axis=0)
            for j in range(4)
        ]
        for d in range(4)
    ]
    right_side = jnp.concatenate(line[40:44], axis=0)
    diagonal = (
        jnp.concatenate([line[PAIR_AT[(i, i)]] for i in range(4)], axis=0) + ATT_PRIOR
    )
    span = count + 256
    zero_halo = jnp.zeros((4, 128), jnp.float32)
    coeff = jnp.concatenate(
        [
            jnp.where(seg > 0, att_left[:, count - 128 :], zero_halo),
            att_ref[...],
            jnp.where(seg < n_att - 1, att_right[:, :128], zero_halo),
        ],
        axis=1,
    )

    def apply(vec):
        image = jnp.zeros_like(vec)
        for d in range(4):
            ahead = vec if d == 0 else pltpu.roll(vec, span - d, 1)
            low = jnp.zeros_like(vec)
            for j in range(4):
                image = image + band[d][j] * ahead[j : j + 1]
                if d > 0:
                    low = low + band[d][j] * vec[j : j + 1]
            if d > 0:
                image = image + pltpu.roll(low, d, 1)
        return image

    right_side = right_side - apply(coeff)
    step = OMEGA * right_side / diagonal
    for _ in range(ITERS - 1):
        step = step + OMEGA * (right_side - apply(step) - ATT_PRIOR * step) / diagonal
    step_ref[...] = step[:, 128 : 128 + count]
    updated = coeff + step
    shifted = jnp.concatenate(
        [
            (updated if j == 0 else pltpu.roll(updated, span - j, 1))[:, 128 : 128 + count]
            for j in range(4)
        ],
        axis=0,
    )
    hot2 = jnp.where(
        lax.broadcasted_iota(jnp.int32, (count, nblock), 0) == knot_ref[...] - seg * count, 1.0, 0.0
    )
    picked = lax.dot_general(
        shifted,
        hot2,
        (((1,), (0,)), ((), ())),
        precision=HIGH,
        preferred_element_type=jnp.float32,
    )
    resid = vt[1]
    for i in range(4):
        knot_sum = jnp.zeros((width, nblock), jnp.float32)
        for j in range(4):
            knot_sum = knot_sum + bt[j] * picked[j * 4 + i : j * 4 + i + 1]
        resid = resid - pt[i] * knot_sum
    rr[...] = (vt[0] * resid).T

    def g_step(g, carry):
        lane_hot, high = hot_pair(g)
        p = spart_ref[:, pl.ds(pl.multiple_of(g * STEP, STEP), STEP)]
        terms = jnp.concatenate(
            [p * row_of(rr, g), jnp.zeros((3, STEP), jnp.float32)], axis=0
        )
        coarse = terms.astype(jnp.bfloat16).astype(jnp.float32)
        both = jnp.concatenate([coarse, terms - coarse], axis=0).astype(jnp.bfloat16)
        got = dot_last(spread([both], high), lane_hot)
        acc_g[0] += got[:, :128]
        acc_g[1] += got[:, 128:]
        return carry

    acc_g[...] = jnp.zeros_like(acc_g)
    lax.fori_loop(0, steps, g_step, 0)
    for c in range(5):
        for half in range(2):
            g_slots[seg, c, :, half * 128 : half * 128 + 128] = (
                acc_g[half, pl.ds(c, LO, stride=16), :]
                + acc_g[half, pl.ds(8 + c, LO, stride=16), :]
            )
    for t in range(1, n_att):
        across(g_slots, g_send, g_recv, t, seg).start()

    def collect(buf, send, recv):
        for t in range(1, n_att):
            across(buf, send, recv, t, seg).wait_send()
            across(buf, send, recv, t, lax.rem(seg + t, n_att)).wait_recv()

    collect(s_slots, s_send, s_recv)

    def summed(buf, c):
        got = buf[0, c]
        for a in range(1, n_att):
            got = got + buf[a, c]
        return got

    entries = [[None] * 5 for _ in range(5)]
    for k in range(3):
        for i in range(5):
            got = summed(s_slots, k * 5 + i)
            other = (i + k) % 5
            if k == 0:
                got = got + SRC_PRIOR
            entries[i][other] = got
            entries[other][i] = got
    factors = {}
    for pivot in range(5):
        for row in range(pivot + 1, 5):
            factor = entries[row][pivot] / entries[pivot][pivot]
            factors[(row, pivot)] = factor
            for column in range(pivot + 1, 5):
                entries[row][column] = entries[row][column] - factor * entries[pivot][column]

    collect(g_slots, g_send, g_recv)
    target = [summed(g_slots, c) for c in range(5)]
    for pivot in range(5):
        for row in range(pivot + 1, 5):
            target[row] = target[row] - factors[(row, pivot)] * target[pivot]
    result = [None] * 5
    for row in reversed(range(5)):
        got = target[row]
        for column in range(row + 1, 5):
            got = got - entries[row][column] * result[column]
        result[row] = got / entries[row][row]
    for c in range(5):
        for a in range(LO):
            out_ref[c : c + 1, a * HI : (a + 1) * HI] = result[c][a : a + 1, :]


def solution(mesh):
    n_src = mesh.shape["src"]
    n_att = mesh.shape["att"]

    def shards(
        attitude,
        obs_value,
        obs_weight,
        obs_time,
        att_partials,
        src_partials,
        obs_source,
        knot_start,
        valid_count,
    ):
        nblock = knot_start.shape[0]
        width = obs_value.shape[0] // nblock
        count = attitude.shape[1]
        per = -(-USED_ROWS // n_src)
        f32 = jnp.float32
        dma = pltpu.SemaphoreType.DMA
        vmem = pl.BlockSpec(memory_space=pltpu.VMEM)
        hbm = pl.BlockSpec(memory_space=pltpu.HBM)
        tall = (width, nblock)
        return pl.pallas_call(
            functools.partial(kernel, n_src, n_att),
            out_shape=(
                jax.ShapeDtypeStruct((4, count), f32),
                jax.ShapeDtypeStruct((5, SRC_DEV), f32),
            ),
            in_specs=[vmem] + [hbm] * 6 + [vmem] * 2,
            out_specs=(vmem, vmem),
            scratch_shapes=[
                pltpu.VMEM((nblock, width), f32),
                pltpu.VMEM((nblock, width), f32),
                pltpu.VMEM((nblock, width), f32),
                pltpu.VMEM((4, nblock * width), f32),
                pltpu.VMEM((5, nblock * width), f32),
                pltpu.VMEM((nblock, width), jnp.int32),
                dma((6,)),
                pltpu.VMEM((4 * nblock, width), f32),
                pltpu.VMEM((2,) + tall, f32),
                pltpu.VMEM((4,) + tall, f32),
                pltpu.VMEM((4,) + tall, f32),
                pltpu.VMEM((nblock, width), f32),
                pltpu.VMEM((nblock, width), f32),
                pltpu.VMEM((14,) + tall, f32),
                pltpu.VMEM((4 * BAND_ROWS, nblock), f32),
                pltpu.VMEM((n_src, per, count + 128), f32),
                pltpu.VMEM((n_src, per, count + 128), f32),
                pltpu.VMEM((n_src, per, count + 128), f32),
                pltpu.VMEM((n_src, per, 256), f32),
                pltpu.VMEM((n_src, per, 128), f32),
                pltpu.VMEM((4, count), f32),
                pltpu.VMEM((4, count), f32),
                pltpu.VMEM((2, LO * 32, 128), f32),
                pltpu.VMEM((2, LO * 16, 128), f32),
                pltpu.VMEM((n_att, 15, LO, HI), f32),
                pltpu.VMEM((n_att, 5, LO, HI), f32),
                dma((n_src,)),
                dma((n_src,)),
                dma((n_src,)),
                dma((n_src,)),
                dma((n_src,)),
                dma((n_src,)),
                dma((n_src,)),
                dma((n_src,)),
                dma((2,)),
                dma((2,)),
                dma((n_att,)),
                dma((n_att,)),
                dma((n_att,)),
                dma((n_att,)),
            ],
            compiler_params=pltpu.CompilerParams(
                collective_id=0,
                has_side_effects=True,
                vmem_limit_bytes=56 * 1024 * 1024,
            ),
        )(
            attitude,
            obs_value.reshape(nblock, width),
            obs_weight.reshape(nblock, width),
            obs_time.reshape(nblock, width),
            att_partials,
            src_partials,
            obs_source.reshape(nblock, width),
            knot_start.reshape(1, nblock),
            valid_count.reshape(1, nblock),
        )

    in_specs = (
        P(None, "att"),
        P(("src", "att")),
        P(("src", "att")),
        P(("src", "att")),
        P(None, ("src", "att")),
        P(None, ("src", "att")),
        P(("src", "att")),
        P(("src", "att")),
        P(("src", "att")),
    )
    out_specs = (P(None, "att"), P(None, "src"))
    return jax.shard_map(shards, mesh=mesh, in_specs=in_specs, out_specs=out_specs, check_vma=False)
```
